32 devices in a mesh: slab: 8 (over z, x), orb: 4 (over y, core).
Axes of the slice: x: 2, y: 2, z: 4, core: 2. Of those that a mesh axis runs over, the one named last changes fastest.
Arguments:
- orbitals: bfloat16 [2048, 128, 256], P(('slab', 'orb')), may hold values from -12 to 12
- region_start: int32 [2048], P(('slab', 'orb')), may hold values from 0 to 1023, as said below
- kin_cross: bfloat16 [256, 256], replicated, may hold values from -0.375 to 0.375
- potential: float32 [1024, 256], P(('slab', 'orb')), may hold values from 0.5 to 2
- pattern: int32 [32, 5], replicated, may hold values from 0 to 31, as said below
Outputs:
- gradient: bfloat16 [2048, 128, 256], P(('slab', 'orb'))
The draws below stay inside these ranges and needn't reach their ends.
Inputs may be any that keep to these rules, and one draw needn't show every extreme that they name: `region_start`: region_start_i - (i // 256) * 128 lies in 0 to 127 and takes both ends within every slab's orbitals; regions continue periodically past the last grid column. `pattern`: row b lists 5 distinct blocks, b among them, all whose orbitals begin in slab b // 4 or the slab before or after it, taken periodically.
All inputs are finite; a program needn't handle non-finite values.
Results may differ from the reference program's by a relative error of at most 0.0085.
Values may be sent and summed in bfloat16 or wider, within the bound.
A program may use at most 128 MiB of HBM per device.

```python
import math
import jax
import jax.numpy as jnp
from jax import lax

C = 256
LW = 128
BLOCK = 64
BLK_SLAB = 4
NNB = 5
ORB_SLAB = 256
NORB = 2048
NBLK = 32
NG = 1024
N_SLAB = 8


def region_offsets(key):
    raw = jax.random.randint(jax.random.fold_in(key, 11), (NORB,), 0, LW, dtype=jnp.int32)
    inside = jnp.arange(NORB, dtype=jnp.int32) % ORB_SLAB
    raw = jnp.where(inside == 0, 0, jnp.where(inside == ORB_SLAB - 1, LW - 1, raw))
    return jnp.arange(NORB, dtype=jnp.int32) // ORB_SLAB * LW + raw


def draw_region_start(key, part):
    return region_offsets(key).astype(jnp.int32)


def draw_orbitals(key, part):
    starts = region_offsets(key)
    columns = (starts[:, None] + jnp.arange(LW, dtype=jnp.int32)[None, :]) % NG
    fields = jax.random.normal(jax.random.fold_in(key, 12), (4, NG, C), jnp.float32)
    weights = 0.5 * jax.random.normal(jax.random.fold_in(key, 13), (NORB, 4), jnp.float32)
    noise = jax.random.normal(jax.random.fold_in(key, 14), (NORB, LW, C), jnp.float32)
    total = noise
    for which in range(4):
        total = total + weights[:, which][:, None, None] * fields[which][columns]
    return jnp.clip(total, -12.0, 12.0).astype(jnp.bfloat16)


def draw_pattern(key, part):
    others = 3 * BLK_SLAB - 1
    keys = jax.random.split(jax.random.fold_in(key, 21), NBLK)
    perms = jax.vmap(lambda single: jax.random.permutation(single, others))(keys).astype(jnp.int32)
    blocks = jnp.arange(NBLK, dtype=jnp.int32)
    self_local = BLK_SLAB + blocks % BLK_SLAB
    mapped = jnp.where(perms >= self_local[:, None], perms + 1, perms)
    chosen = jnp.concatenate([self_local[:, None], mapped[:, :NNB - 1]], axis=1)
    slab_of = blocks // BLK_SLAB
    return (((slab_of[:, None] - 1) * BLK_SLAB + chosen) % NBLK).astype(jnp.int32)


def block_scale(own_key, dims, cuts, smallest, top_value):
    gain, own = 1.0, jax.random.fold_in(own_key, 6)
    for axis_at, blocks in cuts:
        steps = jnp.exp(jax.random.uniform(jax.random.fold_in(own, axis_at), (blocks,), jnp.float32, smallest / len(cuts), top_value / len(cuts)))
        gain = gain * jnp.repeat(steps, dims[axis_at] // blocks).reshape([-1 if axis == axis_at else 1 for axis in range(len(dims))])
    return gain


def normal_values(stream_key, shape, spread, most, held_as=jnp.bfloat16):
    drawn = jax.random.normal(stream_key, shape, jnp.float32) * spread
    return jnp.minimum(jnp.maximum(drawn, -most), most).astype(held_as)


def setup_inputs(seed: int = 0) -> dict:
    splits = jax.random.split(jax.random.key(seed), 6)
    return {
        "orbitals": draw_orbitals(jax.random.fold_in(splits[5], 71), 0),
        "region_start": draw_region_start(jax.random.fold_in(splits[5], 71), 0),
        "kin_cross": normal_values(splits[2], (C, C), C ** -0.5, 0.375),
        "potential": jnp.clip(jnp.exp(math.log(2.0) - 1.3862944 * jax.random.uniform(splits[3], (NG, C), jnp.float32) ** block_scale(splits[3], (NG, C), ((0, 32),), -0.2, 0.2)), 0.5, 2.0),
        "pattern": draw_pattern(jax.random.fold_in(splits[5], 71), 0),
    }


def kinetic_term(values, left_col, right_col, kin_cross):
    widen = values.astype(jnp.float32)
    before = jnp.concatenate([left_col, widen[:, :-1]], axis=1)
    after = jnp.concatenate([widen[:, 1:], right_col], axis=1)
    across = jnp.dot(values.reshape(-1, values.shape[2]), kin_cross, preferred_element_type=jnp.float32)
    across = across.reshape(widen.shape)
    return (0.5 * (2.0 * widen - before - after) + across).astype(jnp.bfloat16)


def place_rows(values, offset):
    length = values.shape[1]
    zero_block = jnp.zeros_like(values)
    padded = jnp.concatenate([zero_block, values, zero_block], axis=1)

    def single(orb_row, begin_at):
        return lax.dynamic_slice_in_dim(orb_row, (length - begin_at).astype(jnp.int32), 2 * length, 0)

    return jax.vmap(single)(padded, offset)


def window_rows(values, offset, length):
    def single(orb_row, begin_at):
        return lax.dynamic_slice_in_dim(orb_row, begin_at.astype(jnp.int32), length, 0)

    return jax.vmap(single)(values, offset)


def reference(orbitals, region_start, kin_cross, potential, pattern):
    norb = orbitals.shape[0]
    owner = jnp.arange(norb, dtype=jnp.int32) // ORB_SLAB
    offset = (region_start - owner * LW).astype(jnp.int32)
    edge = jnp.zeros((norb, 1, C), jnp.float32)
    kinetic = kinetic_term(orbitals, edge, edge, kin_cross)
    phi_buf = place_rows(orbitals, offset).reshape(N_SLAB, ORB_SLAB, 2, LW, C)
    kin_buf = place_rows(kinetic, offset).reshape(N_SLAB, ORB_SLAB, 2, LW, C)
    cover = jnp.any(pattern[:, :, None] == jnp.arange(NBLK, dtype=jnp.int32)[None, None, :], axis=1)
    slab_pot = potential.reshape(N_SLAB, LW, C)
    volume = 1.0 / (LW * C)
    scale = 1.0 / (NNB * BLOCK)
    contract_rows = (((1,), (1,)), ((), ()))
    contract_cols = (((0,), (0,)), ((), ()))
    half_count = ORB_SLAB

    def slab_fields(slab_index):
        before = (slab_index - 1) % N_SLAB
        phi_grid = jnp.concatenate([phi_buf[before][:, 1], phi_buf[slab_index][:, 0]], axis=0)
        kin_grid = jnp.concatenate([kin_buf[before][:, 1], kin_buf[slab_index][:, 0]], axis=0)
        applied = (kin_grid.astype(jnp.float32) + slab_pot[slab_index][None] * phi_grid.astype(jnp.float32)).astype(jnp.bfloat16)
        return phi_grid.reshape(2 * ORB_SLAB, LW * C), applied.reshape(2 * ORB_SLAB, LW * C)

    def partial_pairs(slab_index):
        flat_phi, flat_app = slab_fields(slab_index)
        intersection = lax.dot_general(flat_phi, flat_phi, contract_rows, preferred_element_type=jnp.float32) * volume
        hamilton = lax.dot_general(flat_phi, flat_app, contract_rows, preferred_element_type=jnp.float32) * volume
        return intersection, hamilton

    slab_ids = jnp.arange(N_SLAB, dtype=jnp.int32)
    part_over, part_ham = lax.map(partial_pairs, slab_ids)

    def complete(sums):
        prev_bb = jnp.roll(sums[:, half_count:, half_count:], 1, axis=0)
        next_aa = jnp.roll(sums[:, :half_count, :half_count], -1, axis=0)
        sums = sums.at[:, :half_count, :half_count].add(prev_bb)
        return sums.at[:, half_count:, half_count:].add(next_aa)

    full_over = complete(part_over)
    full_ham = complete(part_ham)

    def gradient_slab(slab_index):
        flat_phi, flat_app = slab_fields(slab_index)
        block_ids = ((slab_index - 1) * BLK_SLAB + jnp.arange(2 * BLK_SLAB, dtype=jnp.int32)) % NBLK
        sub_cover = jnp.take(jnp.take(cover, block_ids, axis=0), block_ids, axis=1).astype(jnp.float32)
        orb_cover = jnp.repeat(jnp.repeat(sub_cover, BLOCK, axis=0), BLOCK, axis=1)
        masked_intersection = (full_over[slab_index] * orb_cover).astype(jnp.bfloat16)
        masked_hamilton = (full_ham[slab_index] * orb_cover).astype(jnp.bfloat16)
        first = lax.dot_general(masked_intersection, flat_app, contract_cols, preferred_element_type=jnp.float32)
        second = lax.dot_general(masked_hamilton, flat_phi, contract_cols, preferred_element_type=jnp.float32)
        return ((first - second) * scale).astype(jnp.bfloat16).reshape(2 * ORB_SLAB, LW, C)

    grads = lax.map(gradient_slab, slab_ids)
    own_part = grads[:, half_count:]
    next_part = jnp.roll(grads[:, :half_count], -1, axis=0)
    buffers = jnp.concatenate([own_part, next_part], axis=2).reshape(norb, 2 * LW, C)
    return window_rows(buffers, offset, LW)
```

```python
import functools

import jax
import jax.numpy as jnp
from jax import lax
from jax.experimental import pallas as pl
from jax.experimental.pallas import tpu as pltpu
from jax.sharding import PartitionSpec as P

BLOCK = 64
CHUNKS = 2
VMEM = 50 * 1024 * 1024
F32 = jnp.float32
BF16 = jnp.bfloat16
ROWS = (((1,), (1,)), ((), ()))
MAJOR = (((1,), (0,)), ((), ()))


def column(refs, at):
    parts = [ref[:, at].reshape(-1, ref.shape[3]) for ref in refs]
    return jnp.concatenate(parts, axis=0)


def kinetic_of(refs, col, place, filt, off, length):
    phi = column(refs, col + 1)
    before = column(refs, col).astype(F32)
    after = column(refs, col + 2).astype(F32)
    zero = jnp.zeros_like(before)
    before = jnp.where(off == place, zero, before)
    last = jnp.where(off == 0.0, F32(length), off) - 1.0
    after = jnp.where(last == place, zero, after)
    wide = phi.astype(F32)
    across = lax.dot_general(phi, filt, MAJOR, preferred_element_type=F32)
    kin = (0.5 * (2.0 * wide - before - after) + across).astype(BF16)
    return wide, kin.astype(F32)


def own_kernel(chunks, length, *refs):
    parts = refs[:chunks]
    off_ref, base_ref, filt_ref, pot_ref, right_ref, sums_ref = refs[chunks:]
    col = pl.program_id(0)
    place = base_ref[0] + col.astype(F32)
    off = off_ref[...]
    wide, kin = kinetic_of(parts, col, place, filt_ref[...], off, length)
    count = wide.shape[0]
    own = off <= place
    zero = jnp.zeros_like(wide)

    @pl.when(col == 0)
    def _():
        sums_ref[...] = jnp.zeros_like(sums_ref)

    total = sums_ref[...]
    for side in range(2):
        app = kin + pot_ref[side, pl.ds(col, 1), :] * wide
        keep = own if side == 0 else jnp.logical_not(own)
        phi_side = jnp.where(keep, wide, zero).astype(BF16)
        app_side = jnp.where(keep, app, zero).astype(BF16)
        right_ref[0, side, :count] = phi_side
        right_ref[0, side, count:] = app_side
        both = jnp.concatenate([phi_side, app_side], axis=0)
        total += lax.dot_general(both, phi_side, ROWS, preferred_element_type=F32)
    sums_ref[...] = total


def other_kernel(chunks, length, *refs):
    parts = refs[:chunks]
    off_ref, base_ref, side_ref, filt_ref, pot_ref, right_ref, left_ref, sums_ref = refs[chunks:]
    col = pl.program_id(0)
    place = base_ref[0] + col.astype(F32)
    off = off_ref[...]
    wide, kin = kinetic_of(parts, col, place, filt_ref[...], off, length)
    count = wide.shape[0]
    side = side_ref[0]
    sign = jnp.where(side == 0, F32(-1.0), F32(1.0))
    keep = (place + 0.5 - off) * sign > 0.0
    zero = jnp.zeros_like(wide)
    app = kin + pot_ref[side, pl.ds(col, 1), :] * wide
    phi_side = jnp.where(keep, wide, zero).astype(BF16)
    app_side = jnp.where(keep, app, zero).astype(BF16)
    left_ref[0, :count] = phi_side
    left_ref[0, count:] = app_side

    @pl.when(col == 0)
    def _():
        sums_ref[...] = jnp.zeros_like(sums_ref)

    sums_ref[...] += lax.dot_general(
        right_ref[0, side], phi_side, ROWS, preferred_element_type=F32
    )


def gradient_kernel(chunks, scale, *refs):
    off_ref, base_ref, side_ref, weight_ref, right_ref, one_ref, two_ref, out_ref = refs
    col = pl.program_id(0)
    place = base_ref[0] + col.astype(F32)
    off = off_ref[...]
    sign = jnp.where(side_ref[0] == 0, F32(1.0), F32(-1.0))
    own = off <= place
    with_one = (place + 0.5 - off) * sign > 0.0

    def product(which, block):
        return lax.dot_general(weight_ref[which], block, MAJOR, preferred_element_type=F32)

    near = jnp.where(own, product(0, right_ref[0, 0]), product(0, right_ref[0, 1]))
    far = jnp.where(with_one, product(1, one_ref[0]), product(2, two_ref[0]))
    grad = ((near + far) * scale).astype(BF16)
    peers, per = out_ref.shape[0], out_ref.shape[2] // chunks
    for chunk in range(chunks):
        for peer in range(peers):
            at = (chunk * peers + peer) * per
            out_ref[peer, 0, chunk * per:(chunk + 1) * per, :] = grad[at:at + per]


def whole(array):
    return pl.BlockSpec(array.shape, lambda col: (0,) * array.ndim)


def per_col(shape, lead=0):
    def index(col):
        return tuple(col if at == lead else 0 for at in range(len(shape)))

    block = tuple(1 if at == lead else size for at, size in enumerate(shape))
    return pl.BlockSpec(block, index)


SMEM = pl.BlockSpec(memory_space=pltpu.SMEM)
PARAMS = pltpu.CompilerParams(vmem_limit_bytes=VMEM)


def window_rows(values, offset, length):
    def single(orb_row, begin_at):
        return lax.dynamic_slice_in_dim(orb_row, begin_at, length, 0)

    return jax.vmap(single)(values, offset)


def per_device(orbitals, region_start, kin_cross, potential, pattern):
    held, length, cross = orbitals.shape
    peers = lax.axis_size("orb")
    slabs = lax.axis_size("slab")
    slab_id = lax.axis_index("slab")
    orb_id = lax.axis_index("orb")
    per_slab = held * peers
    narrow = length // peers
    per = held // CHUNKS
    offset = region_start - slab_id * length

    starts = lax.all_gather(region_start, ("slab", "orb"), axis=0, tiled=True)
    starts = starts.reshape(slabs, per_slab)
    ids = jnp.arange(per_slab, dtype=jnp.int32).reshape(peers, CHUNKS, per)
    ids = ids.transpose(1, 0, 2).reshape(per_slab)
    odd = slab_id % 2
    first = slab_id + 1 - 2 * odd
    second = lax.rem(slab_id - 1 + 2 * odd + slabs, slabs)
    first_side = (1 - odd).astype(jnp.int32)
    groups = [slab_id, first, second]
    offs = []
    for group in groups:
        row = lax.dynamic_index_in_dim(starts, group, 0, keepdims=False) - group * length
        row = row.reshape(peers, CHUNKS, per).transpose(1, 0, 2).reshape(per_slab, 1)
        offs.append(jnp.broadcast_to(row.astype(F32), (per_slab, cross)))
    base = (orb_id * narrow).astype(F32).reshape(1)
    pot_next = lax.ppermute(potential, "slab", [(i, (i - 1) % slabs) for i in range(slabs)])
    pots = jnp.stack([potential, pot_next])

    swap = [(i, i ^ 1) for i in range(slabs)]
    onward = [(i, (i + 2 - 4 * (i % 2)) % slabs) for i in range(slabs)]
    own_parts, one_parts, two_parts = [], [], []
    for chunk in range(CHUNKS):
        rows = slice(chunk * per, (chunk + 1) * per)
        values = orbitals[rows]
        around = jnp.concatenate([values, values, values[:, :2]], axis=1)
        rolled = window_rows(around, length - 1 - offset[rows], length + 2)
        cut = jnp.stack([rolled[:, d * narrow:(d + 1) * narrow + 2] for d in range(peers)])
        cut = cut.transpose(0, 2, 1, 3)
        own_parts.append(lax.all_to_all(cut, "orb", split_axis=0, concat_axis=0, tiled=True))
    for part in own_parts:
        one_parts.append(lax.ppermute(part, "slab", swap))
    for part in one_parts:
        two_parts.append(lax.ppermute(part, "slab", onward))

    right_shape = (narrow, 2, 2 * per_slab, cross)
    left_shape = (narrow, 2 * per_slab, cross)
    sums_shape = (2 * per_slab, per_slab)
    sums_spec = pl.BlockSpec(sums_shape, lambda col: (0, 0))
    product = 2 * per_slab * per_slab * cross * narrow
    right, own_sums = pl.pallas_call(
        functools.partial(own_kernel, CHUNKS, length),
        grid=(narrow,),
        in_specs=[whole(p) for p in own_parts]
        + [whole(offs[0]), SMEM, whole(kin_cross), whole(pots)],
        out_specs=[per_col(right_shape), sums_spec],
        out_shape=[
            jax.ShapeDtypeStruct(right_shape, BF16),
            jax.ShapeDtypeStruct(sums_shape, F32),
        ],
        compiler_params=PARAMS,
        cost_estimate=pl.CostEstimate(
            flops=5 * product, bytes_accessed=22 * 2**20, transcendentals=0
        ),
    )(*own_parts, offs[0], base, kin_cross, pots)

    def other(parts, off, side):
        return pl.pallas_call(
            functools.partial(other_kernel, CHUNKS, length),
            grid=(narrow,),
            in_specs=[whole(p) for p in parts]
            + [whole(off), SMEM, SMEM, whole(kin_cross), whole(pots), per_col(right_shape)],
            out_specs=[per_col(left_shape), sums_spec],
            out_shape=[
                jax.ShapeDtypeStruct(left_shape, BF16),
                jax.ShapeDtypeStruct(sums_shape, F32),
            ],
            compiler_params=PARAMS,
            cost_estimate=pl.CostEstimate(
                flops=3 * product, bytes_accessed=30 * 2**20, transcendentals=0
            ),
        )(*parts, off, base, side.reshape(1), kin_cross, pots, right)

    one_left, one_sums = other(one_parts, offs[1], first_side)
    sums_a = lax.psum(jnp.stack([own_sums, one_sums]), "orb")
    two_left, two_sums = other(two_parts, offs[2], 1 - first_side)
    sums_b = lax.psum(two_sums, "orb")

    blk_slab = per_slab // BLOCK
    mine = ids // BLOCK
    volume = 1.0 / (length * cross)
    weights = []
    for group, sums in zip(groups, (sums_a[0], sums_a[1], sums_b)):
        listed = lax.dynamic_slice_in_dim(pattern, group * blk_slab, blk_slab, 0)
        my_blocks = slab_id * blk_slab + mine
        kept = jnp.any(listed[:, :, None] == my_blocks[None, None, :], axis=1)
        hot = jnp.arange(blk_slab, dtype=jnp.int32)[:, None] == mine[None, :]
        cover = jnp.any(kept[:, :, None] & hot[:, None, :], axis=0).astype(F32)
        inter = (sums[:per_slab] * volume * cover).astype(BF16)
        hamil = (sums[per_slab:] * volume * cover).astype(BF16)
        weights.append(jnp.concatenate([-hamil, inter], axis=1))
    weight = jnp.stack(weights)

    scale = 1.0 / (pattern.shape[1] * BLOCK)
    out_shape = (peers, narrow, held, cross)
    grad = pl.pallas_call(
        functools.partial(gradient_kernel, CHUNKS, scale),
        grid=(narrow,),
        in_specs=[whole(offs[0]), SMEM, SMEM, whole(weight)]
        + [per_col(right_shape), per_col(left_shape), per_col(left_shape)],
        out_specs=per_col(out_shape, 1),
        out_shape=jax.ShapeDtypeStruct(out_shape, BF16),
        compiler_params=PARAMS,
    )(offs[0], base, first_side.reshape(1), weight, right, one_left, two_left)
    owned = lax.all_to_all(grad, "orb", split_axis=0, concat_axis=0, tiled=True)
    owned = owned.reshape(length, held, cross).transpose(1, 0, 2)
    doubled = jnp.concatenate([owned, owned], axis=1)
    return window_rows(doubled, offset, length)


def solution(mesh):
    placed = (
        P(("slab", "orb"), None, None),
        P(("slab", "orb")),
        P(),
        P(("slab", "orb"), None),
        P(),
    )
    return jax.shard_map(
        per_device,
        mesh=mesh,
        in_specs=placed,
        out_specs=P(("slab", "orb"), None, None),
        check_vma=False,
    )
```

```python
import functools

import jax
import jax.numpy as jnp
from jax import lax
from jax.experimental import pallas as pl
from jax.experimental.pallas import tpu as pltpu
from jax.sharding import PartitionSpec as P

BLOCK = 64
CHUNKS = 2
HALVES = 2
VMEM = 50 * 1024 * 1024
F32 = jnp.float32
BF16 = jnp.bfloat16
ROWS = (((1,), (1,)), ((), ()))
MAJOR = (((1,), (0,)), ((), ()))


def column(refs, at):
    parts = [ref[:, at].reshape(-1, ref.shape[3]) for ref in refs]
    return jnp.concatenate(parts, axis=0)


def kinetic_of(refs, col, place, filt, off, length):
    phi = column(refs, col + 1)
    before = column(refs, col).astype(F32)
    after = column(refs, col + 2).astype(F32)
    zero = jnp.zeros_like(before)
    before = jnp.where(off == place, zero, before)
    last = jnp.where(off == 0.0, F32(length), off) - 1.0
    after = jnp.where(last == place, zero, after)
    wide = phi.astype(F32)
    across = lax.dot_general(phi, filt, MAJOR, preferred_element_type=F32)
    kin = (0.5 * (2.0 * wide - before - after) + across).astype(BF16)
    return wide, kin.astype(F32)


def own_kernel(chunks, length, *refs):
    parts = refs[:chunks]
    base_ref, filt_ref, pot_ref, right_ref, sums_ref = refs[chunks:]
    col = pl.program_id(0)
    place = base_ref[0] + col.astype(F32)
    off = column(parts, parts[0].shape[1] - 1).astype(F32)
    wide, kin = kinetic_of(parts, col, place, filt_ref[...], off, length)
    count = wide.shape[0]
    own = off <= place
    zero = jnp.zeros_like(wide)

    @pl.when(col == 0)
    def _():
        sums_ref[...] = jnp.zeros_like(sums_ref)

    total = sums_ref[...]
    for side in range(2):
        app = kin + pot_ref[side, pl.ds(col, 1), :] * wide
        keep = own if side == 0 else jnp.logical_not(own)
        phi_side = jnp.where(keep, wide, zero).astype(BF16)
        app_side = jnp.where(keep, app, zero).astype(BF16)
        right_ref[0, side, :count] = phi_side
        right_ref[0, side, count:] = app_side
        both = jnp.concatenate([phi_side, app_side], axis=0)
        total += lax.dot_general(both, phi_side, ROWS, preferred_element_type=F32)
    sums_ref[...] = total


def other_kernel(chunks, length, *refs):
    parts = refs[:chunks]
    base_ref, side_ref, filt_ref, pot_ref, right_ref, left_ref, sums_ref = refs[chunks:]
    col = pl.program_id(0)
    place = base_ref[0] + col.astype(F32)
    off = column(parts, parts[0].shape[1] - 1).astype(F32)
    wide, kin = kinetic_of(parts, col, place, filt_ref[...], off, length)
    count = wide.shape[0]
    side = side_ref[0]
    sign = jnp.where(side == 0, F32(-1.0), F32(1.0))
    keep = (place + 0.5 - off) * sign > 0.0
    zero = jnp.zeros_like(wide)
    app = kin + pot_ref[side, pl.ds(col, 1), :] * wide
    phi_side = jnp.where(keep, wide, zero).astype(BF16)
    app_side = jnp.where(keep, app, zero).astype(BF16)
    left_ref[0, :count] = phi_side
    left_ref[0, count:] = app_side

    @pl.when(col == 0)
    def _():
        sums_ref[...] = jnp.zeros_like(sums_ref)

    sums_ref[...] += lax.dot_general(
        right_ref[0, side], phi_side, ROWS, preferred_element_type=F32
    )


def near_kernel(chunks, *refs):
    parts = refs[:chunks]
    base_ref, side_ref, weight_ref, right_ref, one_ref, sum_ref = refs[chunks:]
    place = base_ref[0] + pl.program_id(0).astype(F32)
    off = column(parts, parts[0].shape[1] - 1).astype(F32)
    sign = jnp.where(side_ref[0] == 0, F32(1.0), F32(-1.0))
    with_one = (place + 0.5 - off) * sign > 0.0

    def product(which, block):
        return lax.dot_general(weight_ref[which], block, MAJOR, preferred_element_type=F32)

    near = jnp.where(off <= place, product(0, right_ref[0, 0]), product(0, right_ref[0, 1]))
    far = product(1, one_ref[0])
    sum_ref[0] = near + jnp.where(with_one, far, jnp.zeros_like(far))


def far_kernel(chunks, begin, scale, *refs):
    parts = refs[:chunks]
    base_ref, side_ref, weight_ref, sum_ref, two_ref, out_ref = refs[chunks:]
    place = base_ref[0] + (pl.program_id(0) + begin).astype(F32)
    off = column(parts, parts[0].shape[1] - 1).astype(F32)
    sign = jnp.where(side_ref[0] == 0, F32(1.0), F32(-1.0))
    with_one = (place + 0.5 - off) * sign > 0.0
    far = lax.dot_general(weight_ref[...], two_ref[0], MAJOR, preferred_element_type=F32)
    far = jnp.where(with_one, jnp.zeros_like(far), far)
    grad = ((sum_ref[0] + far) * scale).astype(BF16)
    peers, per = out_ref.shape[0], out_ref.shape[2] // chunks
    for chunk in range(chunks):
        for peer in range(peers):
            at = (chunk * peers + peer) * per
            out_ref[peer, 0, chunk * per:(chunk + 1) * per, :] = grad[at:at + per]


def whole(array):
    return pl.BlockSpec(array.shape, lambda col: (0,) * array.ndim)


def offsets_of(array):
    shape = array.shape
    block = (shape[0], 1) + shape[2:]
    return pl.BlockSpec(block, lambda col: (0, shape[1] - 1, 0, 0))


def per_col(shape, lead=0, begin=0):
    def index(col):
        return tuple(col + begin if at == lead else 0 for at in range(len(shape)))

    block = tuple(1 if at == lead else size for at, size in enumerate(shape))
    return pl.BlockSpec(block, index)


SMEM = pl.BlockSpec(memory_space=pltpu.SMEM)
PARAMS = pltpu.CompilerParams(vmem_limit_bytes=VMEM)


def window_rows(values, offset, length):
    def single(orb_row, begin_at):
        return lax.dynamic_slice_in_dim(orb_row, begin_at, length, 0)

    return jax.vmap(single)(values, offset)


def per_device(orbitals, region_start, kin_cross, potential, pattern):
    held, length, cross = orbitals.shape
    peers = lax.axis_size("orb")
    slabs = lax.axis_size("slab")
    slab_id = lax.axis_index("slab")
    orb_id = lax.axis_index("orb")
    per_slab = held * peers
    narrow = length // peers
    per = held // CHUNKS
    offset = region_start - slab_id * length

    ids = jnp.arange(per_slab, dtype=jnp.int32).reshape(peers, CHUNKS, per)
    ids = ids.transpose(1, 0, 2).reshape(per_slab)
    odd = slab_id % 2
    first = slab_id + 1 - 2 * odd
    second = lax.rem(slab_id - 1 + 2 * odd + slabs, slabs)
    first_side = (1 - odd).astype(jnp.int32)
    groups = [slab_id, first, second]
    base = (orb_id * narrow).astype(F32).reshape(1)
    pot_next = lax.ppermute(potential, "slab", [(i, (i - 1) % slabs) for i in range(slabs)])
    pots = jnp.stack([potential, pot_next])

    swap = [(i, i ^ 1) for i in range(slabs)]
    onward = [(i, (i + 2 - 4 * (i % 2)) % slabs) for i in range(slabs)]
    own_parts, one_parts, two_parts = [], [], []
    for chunk in range(CHUNKS):
        rows = slice(chunk * per, (chunk + 1) * per)
        values = orbitals[rows]
        around = jnp.concatenate([values, values, values[:, :2]], axis=1)
        rolled = window_rows(around, length - 1 - offset[rows], length + 2)
        cut = jnp.stack([rolled[:, d * narrow:(d + 1) * narrow + 2] for d in range(peers)])
        told = jnp.broadcast_to(offset[rows].astype(BF16)[None, None, :, None], (peers, 1, per, cross))
        cut = jnp.concatenate([cut.transpose(0, 2, 1, 3), told], axis=1)
        if chunk == 0:
            cut, pots = lax.optimization_barrier((cut, pots))
        own_parts.append(lax.all_to_all(cut, "orb", split_axis=0, concat_axis=0, tiled=True))
    for part in own_parts:
        one_parts.append(lax.ppermute(part, "slab", swap))
    for part in one_parts:
        two_parts.append(lax.ppermute(part, "slab", onward))

    right_shape = (narrow, 2, 2 * per_slab, cross)
    left_shape = (narrow, 2 * per_slab, cross)
    sums_shape = (2 * per_slab, per_slab)
    sums_spec = pl.BlockSpec(sums_shape, lambda col: (0, 0))
    product = 2 * per_slab * per_slab * cross * narrow
    right, own_sums = pl.pallas_call(
        functools.partial(own_kernel, CHUNKS, length),
        grid=(narrow,),
        in_specs=[whole(p) for p in own_parts]
        + [SMEM, whole(kin_cross), whole(pots)],
        out_specs=[per_col(right_shape), sums_spec],
        out_shape=[
            jax.ShapeDtypeStruct(right_shape, BF16),
            jax.ShapeDtypeStruct(sums_shape, F32),
        ],
        compiler_params=PARAMS,
        cost_estimate=pl.CostEstimate(
            flops=5 * product, bytes_accessed=22 * 2**20, transcendentals=0
        ),
    )(*own_parts, base, kin_cross, pots)

    def other(parts, side):
        return pl.pallas_call(
            functools.partial(other_kernel, CHUNKS, length),
            grid=(narrow,),
            in_specs=[whole(p) for p in parts]
            + [SMEM, SMEM, whole(kin_cross), whole(pots), per_col(right_shape)],
            out_specs=[per_col(left_shape), sums_spec],
            out_shape=[
                jax.ShapeDtypeStruct(left_shape, BF16),
                jax.ShapeDtypeStruct(sums_shape, F32),
            ],
            compiler_params=PARAMS,
            cost_estimate=pl.CostEstimate(
                flops=3 * product, bytes_accessed=30 * 2**20, transcendentals=0
            ),
        )(*parts, base, side.reshape(1), kin_cross, pots, right)

    one_left, one_sums = other(one_parts, first_side)
    sums_a = lax.psum(jnp.stack([own_sums, one_sums]), "orb")
    sums_a, two_parts = lax.optimization_barrier((sums_a, two_parts))
    two_left, two_sums = other(two_parts, 1 - first_side)
    sums_b = lax.psum(two_sums, "orb")

    blk_slab = per_slab // BLOCK
    mine = ids // BLOCK
    volume = 1.0 / (length * cross)
    weights = []
    for group, sums in zip(groups, (sums_a[0], sums_a[1], sums_b)):
        listed = lax.dynamic_slice_in_dim(pattern, group * blk_slab, blk_slab, 0)
        my_blocks = slab_id * blk_slab + mine
        kept = jnp.any(listed[:, :, None] == my_blocks[None, None, :], axis=1)
        hot = jnp.arange(blk_slab, dtype=jnp.int32)[:, None] == mine[None, :]
        cover = jnp.any(kept[:, :, None] & hot[:, None, :], axis=0).astype(F32)
        inter = (sums[:per_slab] * volume * cover).astype(BF16)
        hamil = (sums[per_slab:] * volume * cover).astype(BF16)
        weights.append(jnp.concatenate([-hamil, inter], axis=1))
    weight = jnp.stack(weights[:2])

    scale = 1.0 / (pattern.shape[1] * BLOCK)
    told = [offsets_of(p) for p in own_parts]
    side = first_side.reshape(1)
    partial_shape = (narrow, per_slab, cross)
    partial = pl.pallas_call(
        functools.partial(near_kernel, CHUNKS),
        grid=(narrow,),
        in_specs=told + [SMEM, SMEM, whole(weight), per_col(right_shape), per_col(left_shape)],
        out_specs=per_col(partial_shape),
        out_shape=jax.ShapeDtypeStruct(partial_shape, F32),
        compiler_params=PARAMS,
        cost_estimate=pl.CostEstimate(
            flops=3 * product, bytes_accessed=36 * 2**20, transcendentals=0
        ),
    )(*own_parts, base, side, weight, right, one_left)
    half = narrow // HALVES
    out_shape = (peers, half, held, cross)
    landed = []
    for begin in range(0, narrow, half):
        grad = pl.pallas_call(
            functools.partial(far_kernel, CHUNKS, begin, scale),
            grid=(half,),
            in_specs=told
            + [SMEM, SMEM, whole(weights[2])]
            + [per_col(partial_shape, 0, begin), per_col(left_shape, 0, begin)],
            out_specs=per_col(out_shape, 1),
            out_shape=jax.ShapeDtypeStruct(out_shape, BF16),
            compiler_params=PARAMS,
            cost_estimate=pl.CostEstimate(
                flops=product // HALVES, bytes_accessed=10 * 2**20, transcendentals=0
            ),
        )(*own_parts, base, side, weights[2], partial, two_left)
        landed.append(lax.all_to_all(grad, "orb", split_axis=0, concat_axis=0, tiled=True))
    owned = jnp.concatenate(landed, axis=1)
    owned = owned.reshape(length, held, cross).transpose(1, 0, 2)
    doubled = jnp.concatenate([owned, owned], axis=1)
    return window_rows(doubled, offset, length)


def solution(mesh):
    placed = (
        P(("slab", "orb"), None, None),
        P(("slab", "orb")),
        P(),
        P(("slab", "orb"), None),
        P(),
    )
    return jax.shard_map(
        per_device,
        mesh=mesh,
        in_specs=placed,
        out_specs=P(("slab", "orb"), None, None),
        check_vma=False,
    )
```

```python
import functools

import jax
import jax.numpy as jnp
from jax import lax
from jax.experimental import pallas as pl
from jax.experimental.pallas import tpu as pltpu
from jax.sharding import PartitionSpec as P

BLOCK = 64
CHUNKS = 2
HALVES = 4
GROUP = 16
VMEM = 50 * 1024 * 1024
F32 = jnp.float32
BF16 = jnp.bfloat16
ROWS = (((1,), (1,)), ((), ()))
MAJOR = (((1,), (0,)), ((), ()))


def column(refs, at):
    parts = [ref[:, at].reshape(-1, ref.shape[3]) for ref in refs]
    return jnp.concatenate(parts, axis=0)


def kinetic_of(refs, col, place, filt, off, length):
    phi = column(refs, col + 1)
    before = column(refs, col).astype(F32)
    after = column(refs, col + 2).astype(F32)
    zero = jnp.zeros_like(before)
    before = jnp.where(off == place, zero, before)
    last = jnp.where(off == 0.0, F32(length), off) - 1.0
    after = jnp.where(last == place, zero, after)
    wide = phi.astype(F32)
    across = lax.dot_general(phi, filt, MAJOR, preferred_element_type=F32)
    kin = (0.5 * (2.0 * wide - before - after) + across).astype(BF16)
    return wide, kin.astype(F32)


def own_kernel(chunks, length, *refs):
    parts = refs[:chunks]
    base_ref, filt_ref, pot_ref, right_ref, sums_ref = refs[chunks:]
    col = pl.program_id(0)
    place = base_ref[0] + col.astype(F32)
    off = column(parts, parts[0].shape[1] - 1).astype(F32)
    wide, kin = kinetic_of(parts, col, place, filt_ref[...], off, length)
    count = wide.shape[0]
    own = off <= place
    zero = jnp.zeros_like(wide)

    @pl.when(col == 0)
    def _():
        sums_ref[...] = jnp.zeros_like(sums_ref)

    total = sums_ref[...]
    for side in range(2):
        app = kin + pot_ref[side, pl.ds(col, 1), :] * wide
        keep = own if side == 0 else jnp.logical_not(own)
        phi_side = jnp.where(keep, wide, zero).astype(BF16)
        app_side = jnp.where(keep, app, zero).astype(BF16)
        right_ref[0, side, :count] = phi_side
        right_ref[0, side, count:] = app_side
        both = jnp.concatenate([phi_side, app_side], axis=0)
        total += lax.dot_general(both, phi_side, ROWS, preferred_element_type=F32)
    sums_ref[...] = total


def other_kernel(chunks, length, *refs):
    parts = refs[:chunks]
    base_ref, side_ref, filt_ref, pot_ref, right_ref, left_ref, sums_ref = refs[chunks:]
    col = pl.program_id(0)
    place = base_ref[0] + col.astype(F32)
    off = column(parts, parts[0].shape[1] - 1).astype(F32)
    wide, kin = kinetic_of(parts, col, place, filt_ref[...], off, length)
    count = wide.shape[0]
    side = side_ref[0]
    sign = jnp.where(side == 0, F32(-1.0), F32(1.0))
    keep = (place + 0.5 - off) * sign > 0.0
    zero = jnp.zeros_like(wide)
    app = kin + pot_ref[side, pl.ds(col, 1), :] * wide
    phi_side = jnp.where(keep, wide, zero).astype(BF16)
    app_side = jnp.where(keep, app, zero).astype(BF16)
    left_ref[0, :count] = phi_side
    left_ref[0, count:] = app_side

    @pl.when(col == 0)
    def _():
        sums_ref[...] = jnp.zeros_like(sums_ref)

    sums_ref[...] += lax.dot_general(
        right_ref[0, side], phi_side, ROWS, preferred_element_type=F32
    )


def near_kernel(chunks, *refs):
    parts = refs[:chunks]
    base_ref, side_ref, weight_ref, right_ref, one_ref, sum_ref = refs[chunks:]
    place = base_ref[0] + pl.program_id(0).astype(F32)
    off = column(parts, parts[0].shape[1] - 1).astype(F32)
    sign = jnp.where(side_ref[0] == 0, F32(1.0), F32(-1.0))
    with_one = (place + 0.5 - off) * sign > 0.0

    def product(which, block):
        return lax.dot_general(weight_ref[which], block, MAJOR, preferred_element_type=F32)

    near = jnp.where(off <= place, product(0, right_ref[0, 0]), product(0, right_ref[0, 1]))
    far = product(1, one_ref[0])
    sum_ref[0] = near + jnp.where(with_one, far, jnp.zeros_like(far))


def far_kernel(chunks, begin, scale, *refs):
    parts = refs[:chunks]
    base_ref, side_ref, weight_ref, sum_ref, two_ref, out_ref = refs[chunks:]
    place = base_ref[0] + (pl.program_id(0) + begin).astype(F32)
    off = column(parts, parts[0].shape[1] - 1).astype(F32)
    sign = jnp.where(side_ref[0] == 0, F32(1.0), F32(-1.0))
    with_one = (place + 0.5 - off) * sign > 0.0
    far = lax.dot_general(weight_ref[...], two_ref[0], MAJOR, preferred_element_type=F32)
    far = jnp.where(with_one, jnp.zeros_like(far), far)
    grad = ((sum_ref[0] + far) * scale).astype(BF16)
    peers, per = out_ref.shape[0], out_ref.shape[2] // chunks
    for chunk in range(chunks):
        for peer in range(peers):
            at = (chunk * peers + peer) * per
            out_ref[peer, 0, chunk * per:(chunk + 1) * per, :] = grad[at:at + per]


def back_kernel(group, offset_ref, *refs):
    out_ref = refs[-1]
    block = jnp.concatenate([ref[...] for ref in refs[:-1]], axis=1)
    length = out_ref.shape[1]
    block = block.reshape(length, group, out_ref.shape[2]).astype(F32)
    turned = jnp.swapaxes(block, 0, 1)
    for orb in range(group):
        back = lax.rem(length - offset_ref[pl.program_id(0) * group + orb], length)
        out_ref[orb] = pltpu.roll(turned[orb], back, 0).astype(BF16)


def whole(array):
    return pl.BlockSpec(array.shape, lambda col: (0,) * array.ndim)


def offsets_of(array):
    shape = array.shape
    block = (shape[0], 1) + shape[2:]
    return pl.BlockSpec(block, lambda col: (0, shape[1] - 1, 0, 0))


def per_col(shape, lead=0, begin=0):
    def index(col):
        return tuple(col + begin if at == lead else 0 for at in range(len(shape)))

    block = tuple(1 if at == lead else size for at, size in enumerate(shape))
    return pl.BlockSpec(block, index)


SMEM = pl.BlockSpec(memory_space=pltpu.SMEM)
PARAMS = pltpu.CompilerParams(vmem_limit_bytes=VMEM)


def window_rows(values, offset, length):
    def single(orb_row, begin_at):
        return lax.dynamic_slice_in_dim(orb_row, begin_at, length, 0)

    return jax.vmap(single)(values, offset)


def per_device(orbitals, region_start, kin_cross, potential, pattern):
    held, length, cross = orbitals.shape
    peers = lax.axis_size("orb")
    slabs = lax.axis_size("slab")
    slab_id = lax.axis_index("slab")
    orb_id = lax.axis_index("orb")
    per_slab = held * peers
    narrow = length // peers
    per = held // CHUNKS
    offset = region_start - slab_id * length

    ids = jnp.arange(per_slab, dtype=jnp.int32).reshape(peers, CHUNKS, per)
    ids = ids.transpose(1, 0, 2).reshape(per_slab)
    odd = slab_id % 2
    first = slab_id + 1 - 2 * odd
    second = lax.rem(slab_id - 1 + 2 * odd + slabs, slabs)
    first_side = (1 - odd).astype(jnp.int32)
    groups = [slab_id, first, second]
    base = (orb_id * narrow).astype(F32).reshape(1)
    pot_next = lax.ppermute(potential, "slab", [(i, (i - 1) % slabs) for i in range(slabs)])
    pots = jnp.stack([potential, pot_next])

    swap = [(i, i ^ 1) for i in range(slabs)]
    onward = [(i, (i + 2 - 4 * (i % 2)) % slabs) for i in range(slabs)]
    own_parts, one_parts, two_parts = [], [], []
    for chunk in range(CHUNKS):
        rows = slice(chunk * per, (chunk + 1) * per)
        values = orbitals[rows]
        around = jnp.concatenate([values, values, values[:, :2]], axis=1)
        rolled = window_rows(around, length - 1 - offset[rows], length + 2)
        cut = jnp.stack([rolled[:, d * narrow:(d + 1) * narrow + 2] for d in range(peers)])
        told = jnp.broadcast_to(offset[rows].astype(BF16)[None, None, :, None], (peers, 1, per, cross))
        cut = jnp.concatenate([cut.transpose(0, 2, 1, 3), told], axis=1)
        if chunk == 0:
            cut, pots = lax.optimization_barrier((cut, pots))
        own_parts.append(lax.all_to_all(cut, "orb", split_axis=0, concat_axis=0, tiled=True))
    for part in own_parts:
        one_parts.append(lax.ppermute(part, "slab", swap))

    right_shape = (narrow, 2, 2 * per_slab, cross)
    left_shape = (narrow, 2 * per_slab, cross)
    sums_shape = (2 * per_slab, per_slab)
    sums_spec = pl.BlockSpec(sums_shape, lambda col: (0, 0))
    product = 2 * per_slab * per_slab * cross * narrow
    right, own_sums = pl.pallas_call(
        functools.partial(own_kernel, CHUNKS, length),
        grid=(narrow,),
        in_specs=[whole(p) for p in own_parts]
        + [SMEM, whole(kin_cross), whole(pots)],
        out_specs=[per_col(right_shape), sums_spec],
        out_shape=[
            jax.ShapeDtypeStruct(right_shape, BF16),
            jax.ShapeDtypeStruct(sums_shape, F32),
        ],
        compiler_params=PARAMS,
        cost_estimate=pl.CostEstimate(
            flops=5 * product, bytes_accessed=22 * 2**20, transcendentals=0
        ),
    )(*own_parts, base, kin_cross, pots)

    one_parts[0], own_sums = lax.optimization_barrier((one_parts[0], own_sums))
    one_parts[1], right = lax.optimization_barrier((one_parts[1], right))
    for part in one_parts:
        two_parts.append(lax.ppermute(part, "slab", onward))

    def other(parts, side):
        return pl.pallas_call(
            functools.partial(other_kernel, CHUNKS, length),
            grid=(narrow,),
            in_specs=[whole(p) for p in parts]
            + [SMEM, SMEM, whole(kin_cross), whole(pots), per_col(right_shape)],
            out_specs=[per_col(left_shape), sums_spec],
            out_shape=[
                jax.ShapeDtypeStruct(left_shape, BF16),
                jax.ShapeDtypeStruct(sums_shape, F32),
            ],
            compiler_params=PARAMS,
            cost_estimate=pl.CostEstimate(
                flops=3 * product, bytes_accessed=30 * 2**20, transcendentals=0
            ),
        )(*parts, base, side.reshape(1), kin_cross, pots, right)

    one_left, one_sums = other(one_parts, first_side)
    sums_a = lax.psum(jnp.stack([own_sums, one_sums]), "orb")
    sums_a, two_parts = lax.optimization_barrier((sums_a, two_parts))
    two_left, two_sums = other(two_parts, 1 - first_side)
    sums_b = lax.psum(two_sums, "orb")

    blk_slab = per_slab // BLOCK
    mine = ids // BLOCK
    volume = 1.0 / (length * cross)
    weights = []
    for group, sums in zip(groups, (sums_a[0], sums_a[1], sums_b)):
        listed = lax.dynamic_slice_in_dim(pattern, group * blk_slab, blk_slab, 0)
        my_blocks = slab_id * blk_slab + mine
        kept = jnp.any(listed[:, :, None] == my_blocks[None, None, :], axis=1)
        hot = jnp.arange(blk_slab, dtype=jnp.int32)[:, None] == mine[None, :]
        cover = jnp.any(kept[:, :, None] & hot[:, None, :], axis=0).astype(F32)
        inter = (sums[:per_slab] * volume * cover).astype(BF16)
        hamil = (sums[per_slab:] * volume * cover).astype(BF16)
        weights.append(jnp.concatenate([-hamil, inter], axis=1))
    weight = jnp.stack(weights[:2])

    scale = 1.0 / (pattern.shape[1] * BLOCK)
    told = [offsets_of(p) for p in own_parts]
    side = first_side.reshape(1)
    partial_shape = (narrow, per_slab, cross)
    partial = pl.pallas_call(
        functools.partial(near_kernel, CHUNKS),
        grid=(narrow,),
        in_specs=told + [SMEM, SMEM, whole(weight), per_col(right_shape), per_col(left_shape)],
        out_specs=per_col(partial_shape),
        out_shape=jax.ShapeDtypeStruct(partial_shape, F32),
        compiler_params=PARAMS,
        cost_estimate=pl.CostEstimate(
            flops=3 * product, bytes_accessed=36 * 2**20, transcendentals=0
        ),
    )(*own_parts, base, side, weight, right, one_left)
    half = narrow // HALVES
    out_shape = (peers, half, held, cross)
    landed = []
    for begin in range(0, narrow, half):
        grad = pl.pallas_call(
            functools.partial(far_kernel, CHUNKS, begin, scale),
            grid=(half,),
            in_specs=told
            + [SMEM, SMEM, whole(weights[2])]
            + [per_col(partial_shape, 0, begin), per_col(left_shape, 0, begin)],
            out_specs=per_col(out_shape, 1),
            out_shape=jax.ShapeDtypeStruct(out_shape, BF16),
            compiler_params=PARAMS,
            cost_estimate=pl.CostEstimate(
                flops=product // HALVES, bytes_accessed=10 * 2**20, transcendentals=0
            ),
        )(*own_parts, base, side, weights[2], partial, two_left)
        landed.append(lax.all_to_all(grad, "orb", split_axis=0, concat_axis=0, tiled=True))
    group = min(GROUP, held)
    taken = (peers, half, group, cross)
    return pl.pallas_call(
        functools.partial(back_kernel, group),
        grid=(held // group,),
        in_specs=[SMEM] + [pl.BlockSpec(taken, lambda at: (0, 0, at, 0))] * HALVES,
        out_specs=pl.BlockSpec((group, length, cross), lambda at: (at, 0, 0)),
        out_shape=jax.ShapeDtypeStruct(orbitals.shape, BF16),
        compiler_params=PARAMS,
    )(offset, *landed)


def solution(mesh):
    placed = (
        P(("slab", "orb"), None, None),
        P(("slab", "orb")),
        P(),
        P(("slab", "orb"), None),
        P(),
    )
    return jax.shard_map(
        per_device,
        mesh=mesh,
        in_specs=placed,
        out_specs=P(("slab", "orb"), None, None),
        check_vma=False,
    )
```

```python
import functools

import jax
import jax.numpy as jnp
from jax import lax
from jax.experimental import pallas as pl
from jax.experimental.pallas import tpu as pltpu
from jax.sharding import PartitionSpec as P

BLOCK = 64
CHUNKS = 2
HALVES = 4
GROUP = 16
VMEM = 50 * 1024 * 1024
F32 = jnp.float32
BF16 = jnp.bfloat16
ROWS = (((1,), (1,)), ((), ()))
MAJOR = (((1,), (0,)), ((), ()))


def column(refs, at):
    parts = [ref[:, at].reshape(-1, ref.shape[3]) for ref in refs]
    return jnp.concatenate(parts, axis=0)


def kinetic_of(refs, col, place, filt, off, length):
    phi = column(refs, col + 1)
    before = column(refs, col).astype(F32)
    after = column(refs, col + 2).astype(F32)
    zero = jnp.zeros_like(before)
    before = jnp.where(off == place, zero, before)
    last = jnp.where(off == 0.0, F32(length), off) - 1.0
    after = jnp.where(last == place, zero, after)
    wide = phi.astype(F32)
    across = lax.dot_general(phi, filt, MAJOR, preferred_element_type=F32)
    kin = (0.5 * (2.0 * wide - before - after) + across).astype(BF16)
    return wide, kin.astype(F32)


def own_kernel(chunks, length, *refs):
    parts = refs[:chunks]
    base_ref, filt_ref, pot_ref, right_ref, sums_ref = refs[chunks:]
    col = pl.program_id(0)
    place = base_ref[0] + col.astype(F32)
    off = column(parts, parts[0].shape[1] - 1).astype(F32)
    wide, kin = kinetic_of(parts, col, place, filt_ref[...], off, length)
    count = wide.shape[0]
    own = off <= place
    zero = jnp.zeros_like(wide)

    @pl.when(col == 0)
    def _():
        sums_ref[...] = jnp.zeros_like(sums_ref)

    total = sums_ref[...]
    for side in range(2):
        app = kin + pot_ref[side, pl.ds(col, 1), :] * wide
        keep = own if side == 0 else jnp.logical_not(own)
        phi_side = jnp.where(keep, wide, zero).astype(BF16)
        app_side = jnp.where(keep, app, zero).astype(BF16)
        right_ref[0, side, :count] = phi_side
        right_ref[0, side, count:] = app_side
        both = jnp.concatenate([phi_side, app_side], axis=0)
        total += lax.dot_general(both, phi_side, ROWS, preferred_element_type=F32)
    sums_ref[...] = total


def other_kernel(chunks, length, *refs):
    parts = refs[:chunks]
    base_ref, side_ref, filt_ref, pot_ref, right_ref, left_ref, sums_ref = refs[chunks:]
    col = pl.program_id(0)
    place = base_ref[0] + col.astype(F32)
    off = column(parts, parts[0].shape[1] - 1).astype(F32)
    wide, kin = kinetic_of(parts, col, place, filt_ref[...], off, length)
    count = wide.shape[0]
    side = side_ref[0]
    sign = jnp.where(side == 0, F32(-1.0), F32(1.0))
    keep = (place + 0.5 - off) * sign > 0.0
    zero = jnp.zeros_like(wide)
    app = kin + pot_ref[side, pl.ds(col, 1), :] * wide
    phi_side = jnp.where(keep, wide, zero).astype(BF16)
    app_side = jnp.where(keep, app, zero).astype(BF16)
    left_ref[0, :count] = phi_side
    left_ref[0, count:] = app_side

    @pl.when(col == 0)
    def _():
        sums_ref[...] = jnp.zeros_like(sums_ref)

    sums_ref[...] += lax.dot_general(
        right_ref[0, side], phi_side, ROWS, preferred_element_type=F32
    )


def near_kernel(chunks, *refs):
    parts = refs[:chunks]
    base_ref, side_ref, weight_ref, right_ref, one_ref, sum_ref = refs[chunks:]
    place = base_ref[0] + pl.program_id(0).astype(F32)
    off = column(parts, parts[0].shape[1] - 1).astype(F32)
    sign = jnp.where(side_ref[0] == 0, F32(1.0), F32(-1.0))
    with_one = (place + 0.5 - off) * sign > 0.0

    def product(which, block):
        return lax.dot_general(weight_ref[which], block, MAJOR, preferred_element_type=F32)

    near = jnp.where(off <= place, product(0, right_ref[0, 0]), product(0, right_ref[0, 1]))
    far = product(1, one_ref[0])
    sum_ref[0] = near + jnp.where(with_one, far, jnp.zeros_like(far))


def far_kernel(chunks, begin, scale, *refs):
    parts = refs[:chunks]
    base_ref, side_ref, weight_ref, sum_ref, two_ref, out_ref = refs[chunks:]
    place = base_ref[0] + (pl.program_id(0) + begin).astype(F32)
    off = column(parts, parts[0].shape[1] - 1).astype(F32)
    sign = jnp.where(side_ref[0] == 0, F32(1.0), F32(-1.0))
    with_one = (place + 0.5 - off) * sign > 0.0
    far = lax.dot_general(weight_ref[...], two_ref[0], MAJOR, preferred_element_type=F32)
    far = jnp.where(with_one, jnp.zeros_like(far), far)
    grad = ((sum_ref[0] + far) * scale).astype(BF16)
    peers, per = out_ref.shape[0], out_ref.shape[2] // chunks
    for chunk in range(chunks):
        for peer in range(peers):
            at = (chunk * peers + peer) * per
            out_ref[peer, 0, chunk * per:(chunk + 1) * per, :] = grad[at:at + per]


def back_kernel(group, offset_ref, *refs):
    out_ref = refs[-1]
    block = jnp.concatenate([ref[...] for ref in refs[:-1]], axis=1)
    length = out_ref.shape[1]
    block = block.reshape(length, group, out_ref.shape[2]).astype(F32)
    turned = jnp.swapaxes(block, 0, 1)
    for orb in range(group):
        back = lax.rem(length - offset_ref[pl.program_id(0) * group + orb], length)
        out_ref[orb] = pltpu.roll(turned[orb], back, 0).astype(BF16)


def whole(array):
    return pl.BlockSpec(array.shape, lambda col: (0,) * array.ndim)


def offsets_of(array):
    shape = array.shape
    block = (shape[0], 1) + shape[2:]
    return pl.BlockSpec(block, lambda col: (0, shape[1] - 1, 0, 0))


def per_col(shape, lead=0, begin=0):
    def index(col):
        return tuple(col + begin if at == lead else 0 for at in range(len(shape)))

    block = tuple(1 if at == lead else size for at, size in enumerate(shape))
    return pl.BlockSpec(block, index)


SMEM = pl.BlockSpec(memory_space=pltpu.SMEM)
PARAMS = pltpu.CompilerParams(vmem_limit_bytes=VMEM)


def window_rows(values, offset, length):
    def single(orb_row, begin_at):
        return lax.dynamic_slice_in_dim(orb_row, begin_at, length, 0)

    return jax.vmap(single)(values, offset)


def per_device(orbitals, region_start, kin_cross, potential, pattern):
    held, length, cross = orbitals.shape
    peers = lax.axis_size("orb")
    slabs = lax.axis_size("slab")
    slab_id = lax.axis_index("slab")
    orb_id = lax.axis_index("orb")
    per_slab = held * peers
    narrow = length // peers
    per = held // CHUNKS
    offset = region_start - slab_id * length

    ids = jnp.arange(per_slab, dtype=jnp.int32).reshape(peers, CHUNKS, per)
    ids = ids.transpose(1, 0, 2).reshape(per_slab)
    odd = slab_id % 2
    first = slab_id + 1 - 2 * odd
    second = lax.rem(slab_id - 1 + 2 * odd + slabs, slabs)
    first_side = (1 - odd).astype(jnp.int32)
    groups = [slab_id, first, second]
    base = (orb_id * narrow).astype(F32).reshape(1)
    pot_next = lax.ppermute(potential, "slab", [(i, (i - 1) % slabs) for i in range(slabs)])
    pots = jnp.stack([potential, pot_next])

    swap = [(i, i ^ 1) for i in range(slabs)]
    onward = [(i, (i + 2 - 4 * (i % 2)) % slabs) for i in range(slabs)]
    own_parts, one_parts, two_parts = [], [], []
    for chunk in range(CHUNKS):
        rows = slice(chunk * per, (chunk + 1) * per)
        values = orbitals[rows]
        around = jnp.concatenate([values, values, values[:, :2]], axis=1)
        rolled = window_rows(around, length - 1 - offset[rows], length + 2)
        cut = jnp.stack([rolled[:, d * narrow:(d + 1) * narrow + 2] for d in range(peers)])
        told = jnp.broadcast_to(offset[rows].astype(BF16)[None, None, :, None], (peers, 1, per, cross))
        cut = jnp.concatenate([cut.transpose(0, 2, 1, 3), told], axis=1)
        if chunk == 0:
            cut, pots = lax.optimization_barrier((cut, pots))
        own_parts.append(lax.all_to_all(cut, "orb", split_axis=0, concat_axis=0, tiled=True))
    for part in own_parts:
        one_parts.append(lax.ppermute(part, "slab", swap))

    right_shape = (narrow, 2, 2 * per_slab, cross)
    left_shape = (narrow, 2 * per_slab, cross)
    sums_shape = (2 * per_slab, per_slab)
    sums_spec = pl.BlockSpec(sums_shape, lambda col: (0, 0))
    product = 2 * per_slab * per_slab * cross * narrow
    right, own_sums = pl.pallas_call(
        functools.partial(own_kernel, CHUNKS, length),
        grid=(narrow,),
        in_specs=[whole(p) for p in own_parts]
        + [SMEM, whole(kin_cross), whole(pots)],
        out_specs=[per_col(right_shape), sums_spec],
        out_shape=[
            jax.ShapeDtypeStruct(right_shape, BF16),
            jax.ShapeDtypeStruct(sums_shape, F32),
        ],
        compiler_params=PARAMS,
        cost_estimate=pl.CostEstimate(
            flops=5 * product, bytes_accessed=22 * 2**20, transcendentals=0
        ),
    )(*own_parts, base, kin_cross, pots)

    one_parts[0], own_sums = lax.optimization_barrier((one_parts[0], own_sums))
    one_parts[1], right = lax.optimization_barrier((one_parts[1], right))
    for part in one_parts:
        two_parts.append(lax.ppermute(part, "slab", onward))

    def other(parts, side):
        return pl.pallas_call(
            functools.partial(other_kernel, CHUNKS, length),
            grid=(narrow,),
            in_specs=[whole(p) for p in parts]
            + [SMEM, SMEM, whole(kin_cross), whole(pots), per_col(right_shape)],
            out_specs=[per_col(left_shape), sums_spec],
            out_shape=[
                jax.ShapeDtypeStruct(left_shape, BF16),
                jax.ShapeDtypeStruct(sums_shape, F32),
            ],
            compiler_params=PARAMS,
            cost_estimate=pl.CostEstimate(
                flops=3 * product, bytes_accessed=30 * 2**20, transcendentals=0
            ),
        )(*parts, base, side.reshape(1), kin_cross, pots, right)

    own_total = lax.psum(own_sums, "orb")
    own_total, one_parts = lax.optimization_barrier((own_total, one_parts))
    one_left, one_sums = other(one_parts, first_side)
    sums_a = lax.psum(one_sums, "orb")
    sums_a, two_parts = lax.optimization_barrier((sums_a, two_parts))
    two_left, two_sums = other(two_parts, 1 - first_side)
    sums_b = lax.psum(two_sums, "orb")

    blk_slab = per_slab // BLOCK
    mine = ids // BLOCK
    volume = 1.0 / (length * cross)
    weights = []
    for group, sums in zip(groups, (own_total, sums_a, sums_b)):
        listed = lax.dynamic_slice_in_dim(pattern, group * blk_slab, blk_slab, 0)
        my_blocks = slab_id * blk_slab + mine
        kept = jnp.any(listed[:, :, None] == my_blocks[None, None, :], axis=1)
        hot = jnp.arange(blk_slab, dtype=jnp.int32)[:, None] == mine[None, :]
        cover = jnp.any(kept[:, :, None] & hot[:, None, :], axis=0).astype(F32)
        inter = (sums[:per_slab] * volume * cover).astype(BF16)
        hamil = (sums[per_slab:] * volume * cover).astype(BF16)
        weights.append(jnp.concatenate([-hamil, inter], axis=1))
    weight = jnp.stack(weights[:2])

    scale = 1.0 / (pattern.shape[1] * BLOCK)
    told = [offsets_of(p) for p in own_parts]
    side = first_side.reshape(1)
    partial_shape = (narrow, per_slab, cross)
    partial = pl.pallas_call(
        functools.partial(near_kernel, CHUNKS),
        grid=(narrow,),
        in_specs=told + [SMEM, SMEM, whole(weight), per_col(right_shape), per_col(left_shape)],
        out_specs=per_col(partial_shape),
        out_shape=jax.ShapeDtypeStruct(partial_shape, F32),
        compiler_params=PARAMS,
        cost_estimate=pl.CostEstimate(
            flops=3 * product, bytes_accessed=36 * 2**20, transcendentals=0
        ),
    )(*own_parts, base, side, weight, right, one_left)
    half = narrow // HALVES
    out_shape = (peers, half, held, cross)
    landed = []
    for begin in range(0, narrow, half):
        grad = pl.pallas_call(
            functools.partial(far_kernel, CHUNKS, begin, scale),
            grid=(half,),
            in_specs=told
            + [SMEM, SMEM, whole(weights[2])]
            + [per_col(partial_shape, 0, begin), per_col(left_shape, 0, begin)],
            out_specs=per_col(out_shape, 1),
            out_shape=jax.ShapeDtypeStruct(out_shape, BF16),
            compiler_params=PARAMS,
            cost_estimate=pl.CostEstimate(
                flops=product // HALVES, bytes_accessed=10 * 2**20, transcendentals=0
            ),
        )(*own_parts, base, side, weights[2], partial, two_left)
        landed.append(lax.all_to_all(grad, "orb", split_axis=0, concat_axis=0, tiled=True))
    group = min(GROUP, held)
    taken = (peers, half, group, cross)
    return pl.pallas_call(
        functools.partial(back_kernel, group),
        grid=(held // group,),
        in_specs=[SMEM] + [pl.BlockSpec(taken, lambda at: (0, 0, at, 0))] * HALVES,
        out_specs=pl.BlockSpec((group, length, cross), lambda at: (at, 0, 0)),
        out_shape=jax.ShapeDtypeStruct(orbitals.shape, BF16),
        compiler_params=PARAMS,
    )(offset, *landed)


def solution(mesh):
    placed = (
        P(("slab", "orb"), None, None),
        P(("slab", "orb")),
        P(),
        P(("slab", "orb"), None),
        P(),
    )
    return jax.shard_map(
        per_device,
        mesh=mesh,
        in_specs=placed,
        out_specs=P(("slab", "orb"), None, None),
        check_vma=False,
    )
```
